256 devices in a mesh: dp: 64 (over x, y, z_hi), tensor: 4 (over z_lo, core).
Axes of the slice: x: 4, y: 4, z: 8 (z_hi: 4, z_lo: 2; z = z_hi * 2 + z_lo), core: 2. Of those that a mesh axis runs over, the one named last changes fastest.
Arguments:
- hidden: bfloat16 [128, 256, 4096], P('dp', None, 'tensor'), may hold values from -6 to 6
- targets: int32 [128, 256], P('dp'), may hold values from 0 to 511
- lengths: int32 [128], P('dp'), may hold values from 1 to 256, 16384 in all
- conv_filter: bfloat16 [3, 4096], P(None, 'tensor'), may hold values from -3 to 3
- proj_weight: bfloat16 [4096, 4096], P('tensor'), may hold values from -0.09375 to 0.09375
- unembed: bfloat16 [512, 4096], P(None, 'tensor'), may hold values from -0.140625 to 0.140625
- proj_in: bfloat16 [4096, 64], P('tensor'), may hold values from -0.09375 to 0.09375
- proj_out: bfloat16 [4096, 64], P('tensor'), may hold values from -0.09375 to 0.09375
- query_grads: bfloat16 [1024, 4096], P('dp', 'tensor'), may hold values from -6 to 6
Outputs:
- scores: float32 [128, 1024], P('dp')
The draws below stay inside these ranges and needn't reach their ends.
Inputs may be any that keep to these rules, and one draw needn't show every extreme that they name: `lengths`: some row has exactly 256 live tokens.
All inputs are finite; a program needn't handle non-finite values. No bound on the sum of `lengths` on one device may be relied on, other than what follows from the above.
Results may differ from the reference program's by a relative error of at most 0.0075.
Values may be sent and summed in bfloat16 or wider, within the bound.
A program may use at most 64 MiB of HBM per device.

```python
import math
import jax
import jax.numpy as jnp
import numpy as np
from jax import lax

D = 4096
VOCAB = 512
RANK = 64
LEN = 256
ROWS = 128
QUERIES = 1024


def draw_unembed(key, part):
    key = jax.random.fold_in(key, 11)
    key_shared, key_mixing, key_spread = jax.random.split(key, 3)
    mixing = jax.random.uniform(key_mixing, (VOCAB, 1), jnp.float32, 0.0, 2.0)
    shared = jnp.clip(jax.random.normal(key_shared, (D,), jnp.float32), -3.0, 3.0)
    spread = jnp.clip(jax.random.normal(key_spread, (VOCAB, D), jnp.float32), -3.0, 3.0)
    values = (mixing * shared[None, :] + spread) * (1.0 / math.sqrt(D))
    return values.astype(jnp.bfloat16)


def set_ends(result, stream_key, least, high):
    dims = result.shape
    place = [jax.random.randint(jax.random.fold_in(stream_key, axis), (), 0, dims[axis]) for axis in range(len(dims))]
    result = result.at[tuple(place)].set(least)
    longest = dims.index(max(dims))
    place[longest] = (place[longest] + 1) % dims[longest]
    return result.at[tuple(place)].set(high)


def levels(rng, dims, cuts, low, largest):
    level = 1.0
    for dim, shards_of in cuts:
        steps = jax.random.uniform(jax.random.fold_in(jax.random.fold_in(rng, 6), dim), (shards_of,), jnp.float32, low / len(cuts), largest / len(cuts))
        level = level * jnp.repeat(jnp.exp(steps), dims[dim] // shards_of).reshape((-1,) + (1,) * (len(dims) - 1 - dim))
    return level


def length_profile(amount, total, most, lean):
    loads = [(1 << 20) // math.isqrt(rank ** lean) + 1 for rank in range(2, amount + 1)]
    surplus, counts = total - most - (amount - 1), [1] * (amount - 1)
    while surplus > 0:
        candidates = [i for i in range(amount - 1) if counts[i] < most]
        mass, budget = sum([loads[i] for i in candidates]), surplus
        for i in candidates:
            addition = min(most - counts[i], max(1, budget * loads[i] // mass), surplus)
            counts[i] = counts[i] + addition
            surplus = surplus - addition
    return np.array([most] + counts)


def ragged_sizes(own_key, count, total, bound, skew):
    if count == 2:
        one = jax.random.randint(own_key, (), max(1, total - bound), min(bound, total - 1) + 1)
        return jnp.stack([one, total - one])
    sizes = jnp.asarray(length_profile(count, total, bound, skew), jnp.int32)
    twos = (count - 1) // 2
    giver, receiver = sizes[1:1 + 2 * twos:2], sizes[2:2 + 2 * twos:2]
    room = jnp.minimum(giver - 1, bound - receiver)
    moved = jax.random.randint(jax.random.fold_in(own_key, 1), (twos,), 0, 1 << 20) % (room + 1)
    sizes = sizes.at[1:1 + 2 * twos:2].set(giver - moved).at[2:2 + 2 * twos:2].set(receiver + moved)
    return sizes[jax.random.permutation(jax.random.fold_in(own_key, 2), count)]


def scatter_about(rng, shape, deviation, most, cuts=(), held_as=jnp.bfloat16):
    result = deviation * jax.random.normal(rng, shape, jnp.float32)
    if cuts:
        result = result * levels(rng, shape, cuts, -0.22, 0.18)
    return jnp.clip(result, -most, most).astype(held_as)


def setup_inputs(seed: int = 0) -> dict:
    keys = jax.random.split(jax.random.key(seed), 10)
    return {
        "hidden": scatter_about(keys[0], (ROWS, LEN, D), 1.0, 6.0, ((0, 64), (2, 4))),
        "targets": set_ends(jax.random.randint(keys[1], (ROWS, LEN), 0, VOCAB), jax.random.fold_in(keys[1], 1), 0, VOCAB - 1).astype(jnp.int32),
        "lengths": ragged_sizes(keys[2], ROWS, ROWS * LEN // 2, LEN, 2).astype(jnp.int32),
        "conv_filter": scatter_about(keys[3], (3, D), 0.6, 3.0, ((1, 4),)),
        "proj_weight": scatter_about(keys[4], (D, D), D ** -0.5, 0.09375, ((0, 4),)),
        "unembed": draw_unembed(jax.random.fold_in(keys[9], 71), 0),
        "proj_in": scatter_about(keys[6], (D, RANK), D ** -0.5, 0.09375, ((0, 4),)),
        "proj_out": scatter_about(keys[7], (D, RANK), D ** -0.5, 0.09375, ((0, 4),)),
        "query_grads": scatter_about(keys[8], (QUERIES, RANK * RANK), 1.0, 6.0, ((0, 64), (1, 4))),
    }


eps = 1e-06

def short_conv(hidden, conv_filter):
    values = hidden.astype(jnp.float32)
    taps = conv_filter.astype(jnp.float32)
    zero = jnp.zeros_like(values[..., :1, :])
    first = jnp.concatenate([zero, values[..., :-1, :]], axis=-2)
    second = jnp.concatenate([zero, zero, values[..., :-2, :]], axis=-2)
    return (taps[0] * values + taps[1] * first + taps[2] * second).astype(jnp.bfloat16)

def wide_dot(left, right):
    return jnp.dot(left.astype(jnp.float32), right.astype(jnp.float32), precision=lax.Precision.HIGHEST, preferred_element_type=jnp.float32)

def one_row(item, conv_filter, proj_weight, unembed, proj_in, proj_out):
    row_hidden, row_targets, row_length = item
    mixed = short_conv(row_hidden, conv_filter)
    layer_out = wide_dot(mixed, proj_weight)
    layer_low = layer_out.astype(jnp.bfloat16)
    logits = wide_dot(layer_low, unembed.T)
    expo = jnp.exp(logits)
    prob = expo / lax.optimization_barrier(jnp.sum(expo, axis=1, keepdims=True))
    live = (jnp.arange(LEN) < row_length).astype(jnp.float32)
    onehot = (jnp.arange(VOCAB)[None, :] == row_targets[:, None]).astype(jnp.float32)
    grad_logits = ((prob - onehot) * live[:, None]).astype(jnp.bfloat16)
    grad_out = wide_dot(grad_logits, unembed).astype(jnp.bfloat16)
    side_in = wide_dot(mixed, proj_in)
    side_out = wide_dot(grad_out, proj_out)
    row_grad = wide_dot(side_in.T, side_out).reshape(RANK * RANK)
    row_norm = jnp.sum(row_grad * row_grad)
    return (row_grad.astype(jnp.bfloat16), row_norm)

def reference(hidden, targets, lengths, conv_filter, proj_weight, unembed, proj_in, proj_out, query_grads):
    row_low, row_norm = lax.map(lambda item: one_row(item, conv_filter, proj_weight, unembed, proj_in, proj_out), (hidden, targets, lengths))
    inner = wide_dot(row_low, query_grads.T)
    return inner / jnp.sqrt(row_norm + eps)[:, None]
```

```python
import functools

import jax
import jax.numpy as jnp
from jax import lax
from jax.experimental import pallas as pl
from jax.experimental.pallas import tpu as pltpu
from jax.sharding import PartitionSpec as P

EPS = 1e-06
MESH = pl.DeviceIdType.MESH
F32 = jnp.float32
BF16 = jnp.bfloat16

LOCAL = 512
WIDTH = 1024
SIDE = 64
ROWS = LOCAL + SIDE
BLOCKS = 4
BLOCK = LOCAL // BLOCKS
HALF = BLOCK // 2


def nt(left, right, precision=None):
    return lax.dot_general(
        left, right, (((1,), (1,)), ((), ())), precision=precision, preferred_element_type=F32
    )


def kernel(
    hidden,
    targets,
    lengths,
    conv_filter,
    proj_weight,
    unembed,
    proj_in_t,
    proj_out_t,
    queries,
    out,
    held,
    mixed,
    weight,
    words,
    side_in_w,
    side_out_w,
    folded,
    folded_low,
    up_part,
    up_sib,
    up_chip,
    up_far,
    logits_full,
    logits_low,
    from_sib,
    to_far,
    from_far,
    side_t,
    query_all,
    grad_out,
    grad_all,
    grad_rows,
    score_out,
    score_all,
    local_sem,
    uz_send,
    uz_recv,
    us_send,
    us_recv,
    uf_send,
    uf_recv,
    up_send,
    up_recv,
    a_send,
    a_recv,
    b_send,
    b_recv,
    q_send,
    q_recv,
    g_send,
    g_recv,
    s_send,
    s_recv,
):
    dp = lax.axis_index("dp")
    tensor = lax.axis_index("tensor")
    plane, zh = dp // 4, dp % 4
    zl, core = tensor // 2, tensor % 2
    me = zh * 4 + tensor
    sib = (dp, zl * 2 + 1 - core)
    near = (dp, (1 - zl) * 2 + core)
    far = (plane * 4 + (zh + 2 * zl + 3) % 4, (1 - zl) * 2 + core)

    def column(place):
        return (plane * 4 + place // 4, place % 4)

    def in_plane(place):
        return (place * 4 + zh, tensor)

    def remote(src, dst, send, recv, device):
        return pltpu.make_async_remote_copy(
            src_ref=src, dst_ref=dst, send_sem=send, recv_sem=recv, device_id=device, device_id_type=MESH
        )

    barrier = pltpu.get_barrier_semaphore()
    for step in range(1, 16):
        pl.semaphore_signal(barrier, inc=1, device_id=column((me + step) % 16), device_id_type=MESH)
        pl.semaphore_signal(barrier, inc=1, device_id=in_plane((plane + step) % 16), device_id_type=MESH)

    own_slices = (tensor, zl * 2 + 1 - core, (1 - zl) * 2 + core, (1 - zl) * 2 + 1 - core)
    loads = [
        pltpu.make_async_copy(hidden, held, local_sem.at[0]),
        pltpu.make_async_copy(unembed, words.at[0], local_sem.at[1]),
        pltpu.make_async_copy(proj_out_t, side_out_w, local_sem.at[2]),
        pltpu.make_async_copy(proj_in_t, side_in_w, local_sem.at[3]),
    ] + [
        pltpu.make_async_copy(
            proj_weight.at[:, pl.ds(pl.multiple_of(own_slices[i] * WIDTH, WIDTH), WIDTH)],
            weight.at[i],
            local_sem.at[4 + i],
        )
        for i in range(4)
    ] + [
        pltpu.make_async_copy(
            queries, query_all.at[pl.ds(pl.multiple_of(plane * 16, 16), 16)], local_sem.at[8]
        )
    ]
    for load in loads:
        load.start()

    pl.semaphore_wait(barrier, 30)

    sends = []
    to_sib = remote(unembed, words.at[1], us_send, us_recv, sib)
    word_copies = []
    for b in range(BLOCKS):
        pair = []
        for side, device in enumerate((near, far)):
            rows = pl.ds(b * BLOCK + side * HALF, HALF)
            copy = remote(
                unembed.at[rows], words.at[2, rows], uz_send.at[b, side], uz_recv.at[b, side], device
            )
            copy.start()
            pair.append(copy)
        word_copies.append(pair)
        sends.extend(pair)
        if b == 0:
            to_sib.start()
    sends.append(to_sib)

    query_copies = []
    for step in range(1, 16):
        copy = remote(
            queries,
            query_all.at[pl.ds(pl.multiple_of(plane * 16, 16), 16)],
            q_send.at[step],
            q_recv.at[step],
            in_plane((plane + step) % 16),
        )
        copy.start()
        query_copies.append(copy)
    sends.extend(query_copies)

    loads[0].wait()
    chunk = 256
    first_row = lax.broadcasted_iota(jnp.int32, (256, chunk), 0)

    def convolve(i, carry):
        row = i // (WIDTH // chunk)
        columns = pl.ds(pl.multiple_of((i % (WIDTH // chunk)) * chunk, chunk), chunk)
        values = held[row, :, columns].astype(F32)
        taps = conv_filter[:, columns].astype(F32)
        first = jnp.where(first_row < 1, 0.0, pltpu.roll(values, 1, 0))
        second = jnp.where(first_row < 2, 0.0, pltpu.roll(values, 2, 0))
        result = taps[0:1] * values + taps[1:2] * first + taps[2:3] * second
        mixed[pl.ds(pl.multiple_of(row * 256, 256), 256), columns] = result.astype(BF16)
        return carry

    lax.fori_loop(0, 2 * (WIDTH // chunk), convolve, 0)

    loads[1].wait()
    loads[2].wait()
    up_part[...] = nt(side_out_w[...], words[0])
    up_to_sib = remote(up_part, up_sib, up_send.at[0], up_recv.at[0], sib)
    up_to_sib.start()
    sends.append(up_to_sib)

    loads[4].wait()
    folded[...] = nt(words[0], weight[0])

    loads[3].wait()

    def put(rows, part):
        for quarter in range(4):
            logits_full[quarter % 2, quarter // 2, rows] = part[:, quarter * 128 : (quarter + 1) * 128]
            logits_low[quarter % 2, quarter // 2, rows] = part[:, quarter * 128 : (quarter + 1) * 128].astype(
                BF16
            )

    def send_a(index, rows):
        copy = remote(
            logits_low.at[1 - core, :, rows], from_sib.at[:, rows], a_send.at[index], a_recv.at[index], sib
        )
        copy.start()
        sends.append(copy)
        return copy

    def send_b(index, rows, copy):
        copy.wait_recv()
        chip = logits_full[core, 1 - zl, rows] + from_sib[1 - zl, rows].astype(F32)
        to_far[rows] = chip.astype(BF16)
        result = remote(to_far.at[rows], from_far.at[rows], b_send.at[index], b_recv.at[index], near)
        result.start()
        sends.append(result)
        return result

    side_rows = pl.ds(LOCAL, SIDE)
    put(side_rows, nt(side_in_w[...], mixed[...]))
    side_a = send_a(BLOCKS, side_rows)

    up_to_sib.wait_recv()
    up_chip[...] = up_part[...] + up_sib[...]
    up_copies = []
    for side, device in enumerate((near, far)):
        rows = pl.ds(side * (SIDE // 2), SIDE // 2)
        copy = remote(up_chip.at[rows], up_far.at[rows], up_send.at[1 + side], up_recv.at[1 + side], device)
        copy.start()
        up_copies.append(copy)
    sends.extend(up_copies)

    to_sib.wait_recv()
    loads[5].wait()
    folded[...] += nt(words[1], weight[1])
    b_copies = [send_b(BLOCKS, side_rows, side_a)]

    loads[6].wait()
    loads[7].wait()
    previous = None
    for b in range(BLOCKS):
        rows = pl.ds(b * BLOCK, BLOCK)
        for copy in word_copies[b]:
            copy.wait_recv()
        forward = remote(words.at[2, rows], words.at[3, rows], uf_send.at[b], uf_recv.at[b], sib)
        forward.start()
        sends.append(forward)
        part = folded[rows] + nt(words[2, rows], weight[2])
        if previous is not None:
            b_copies.append(send_b(*previous))
        forward.wait_recv()
        folded_low[rows] = (part + nt(words[3, rows], weight[3])).astype(BF16)
        put(rows, nt(folded_low[rows], mixed[...]))
        previous = (b, rows, send_a(b, rows))
    b_copies.append(send_b(*previous))

    for copy in up_copies:
        copy.wait_recv()
    up = (up_chip[...] + up_far[...]).astype(BF16)
    for copy in b_copies:
        copy.wait_recv()
    total = logits_full[core, zl] + from_sib[zl].astype(F32) + from_far[...].astype(F32)
    expo = jnp.exp(total[:LOCAL])
    prob = expo / jnp.sum(expo, axis=0, keepdims=True)
    place = lax.broadcasted_iota(jnp.int32, (1, 128), 1) + core * 128
    live = (place < lengths[zl]).astype(F32)
    ids = [jnp.where(zl == 0, targets[0:1, i : i + 128], targets[1:2, i : i + 128]) for i in (0, 128)]
    target = jnp.where(core == 0, ids[0], ids[1])
    onehot = (lax.broadcasted_iota(jnp.int32, (LOCAL, 128), 0) == target).astype(F32)
    grad_logits = ((prob - onehot) * live).astype(BF16)
    side_out = jnp.dot(up, grad_logits, preferred_element_type=F32)
    side_t[...] = total[LOCAL:]
    even = nt(side_t[pl.ds(0, SIDE // 2, stride=2), :], side_out, lax.Precision.HIGHEST)
    odd = nt(side_t[pl.ds(1, SIDE // 2, stride=2), :], side_out, lax.Precision.HIGHEST)
    row_grad = jnp.concatenate([even, odd], axis=1)
    for share in range(4):
        grad_out[share] = row_grad[share * 8 : (share + 1) * 8]

    grad_all[me] = grad_out[tensor]
    grad_copies = []
    for step in range(1, 16):
        place = (me + step) % 16
        copy = remote(grad_out.at[place % 4], grad_all.at[me], g_send.at[step], g_recv.at[step], column(place))
        copy.start()
        grad_copies.append(copy)
    sends.extend(grad_copies)
    for copy in query_copies:
        copy.wait_recv()
    loads[8].wait()
    for copy in grad_copies:
        copy.wait_recv()

    norms = []
    for row in range(8):
        whole = grad_all[2 * row] + grad_all[2 * row + 1]
        grad_rows[pl.ds(row * 8, 8)] = whole
        norms.append(jnp.sum(whole * whole, axis=(0, 1), keepdims=True))
    flat = jnp.concatenate([grad_rows[pl.ds(i, 8, stride=8), :] for i in range(8)], axis=1).astype(BF16)
    scores = nt(flat, query_all[...])
    for row in range(8):
        for half in range(2):
            score_out[row // 2, pl.ds((row % 2) * 2 + half, 1)] = scores[
                row : row + 1, half * 128 : (half + 1) * 128
            ]
            score_out[row // 2, pl.ds(4 + (row % 2) * 2 + half, 1)] = jnp.broadcast_to(norms[row], (1, 128))

    score_all[me] = score_out[zh]
    score_copies = []
    for step in range(1, 16):
        place = (me + step) % 16
        copy = remote(score_out.at[place // 4], score_all.at[me], s_send.at[step], s_recv.at[step], column(place))
        copy.start()
        score_copies.append(copy)
    sends.extend(score_copies)
    for copy in score_copies:
        copy.wait_recv()

    sums = [score_all[4 * i] + score_all[4 * i + 1] + score_all[4 * i + 2] + score_all[4 * i + 3] for i in range(4)]
    scale = jnp.sqrt(sums[0][4:8] + EPS)
    lane = lax.broadcasted_iota(jnp.int32, (8, 128), 1)
    for k in range(4):
        line = jnp.zeros((8, 128), F32)
        for i in range(4):
            for odd_one in range(2):
                source = 32 * k + 16 * odd_one
                target_lane = 64 * odd_one + 16 * i
                shift = (target_lane - source) % 128
                moved = pltpu.roll(sums[i], shift, 1) if shift else sums[i]
                line = jnp.where((lane >= target_lane) & (lane < target_lane + 16), moved, line)
        line = line[0:4] / scale
        for row in range(2):
            for half in range(2):
                out[pl.ds(row, 1), pl.ds(128 * (4 * half + k), 128)] = line[2 * row + half : 2 * row + half + 1]

    for copy in sends:
        copy.wait_send()


def per_device(hidden, targets, lengths, conv_filter, proj_weight, unembed, proj_in, proj_out, query_grads):
    hbm = pl.BlockSpec(memory_space=pltpu.HBM)
    vmem = pl.BlockSpec(memory_space=pltpu.VMEM)
    smem = pl.BlockSpec(memory_space=pltpu.SMEM)
    dma = pltpu.SemaphoreType.DMA
    scratch = [
        pltpu.VMEM((2, 256, WIDTH), BF16),
        pltpu.VMEM((LOCAL, WIDTH), BF16),
        pltpu.VMEM((4, WIDTH, WIDTH), BF16),
        pltpu.VMEM((4, LOCAL, WIDTH), BF16),
        pltpu.VMEM((SIDE, WIDTH), BF16),
        pltpu.VMEM((SIDE, WIDTH), BF16),
        pltpu.VMEM((LOCAL, WIDTH), F32),
        pltpu.VMEM((LOCAL, WIDTH), BF16),
        pltpu.VMEM((SIDE, LOCAL), F32),
        pltpu.VMEM((SIDE, LOCAL), F32),
        pltpu.VMEM((SIDE, LOCAL), F32),
        pltpu.VMEM((SIDE, LOCAL), F32),
        pltpu.VMEM((2, 2, ROWS, 128), F32),
        pltpu.VMEM((2, 2, ROWS, 128), BF16),
        pltpu.VMEM((2, ROWS, 128), BF16),
        pltpu.VMEM((ROWS, 128), BF16),
        pltpu.VMEM((ROWS, 128), BF16),
        pltpu.VMEM((SIDE, 128), F32),
        pltpu.VMEM((256, WIDTH), BF16),
        pltpu.VMEM((4, 8, 128), F32),
        pltpu.VMEM((16, 8, 128), F32),
        pltpu.VMEM((64, 128), F32),
        pltpu.VMEM((4, 8, 128), F32),
        pltpu.VMEM((16, 8, 128), F32),
        dma((9,)),
        dma((BLOCKS, 2)),
        dma((BLOCKS, 2)),
        dma,
        dma,
        dma((BLOCKS,)),
        dma((BLOCKS,)),
        dma((3,)),
        dma((3,)),
        dma((BLOCKS + 1,)),
        dma((BLOCKS + 1,)),
        dma((BLOCKS + 1,)),
        dma((BLOCKS + 1,)),
        dma((16,)),
        dma((16,)),
        dma((16,)),
        dma((16,)),
        dma((16,)),
        dma((16,)),
    ]
    return pl.pallas_call(
        kernel,
        out_shape=jax.ShapeDtypeStruct((2, 1024), F32),
        in_specs=[hbm, vmem, smem, vmem, hbm, hbm, hbm, hbm, hbm],
        out_specs=vmem,
        scratch_shapes=scratch,
        compiler_params=pltpu.CompilerParams(
            collective_id=0, has_side_effects=True, vmem_limit_bytes=48 * 1024 * 1024
        ),
        name="attribution",
    )(hidden, targets, lengths, conv_filter, proj_weight, unembed, proj_in.T, proj_out.T, query_grads)


def solution(mesh):
    in_specs = (
        P("dp", None, "tensor"),
        P("dp", None),
        P("dp"),
        P(None, "tensor"),
        P("tensor", None),
        P(None, "tensor"),
        P("tensor", None),
        P("tensor", None),
        P("dp", "tensor"),
    )
    return jax.shard_map(
        per_device, mesh=mesh, in_specs=in_specs, out_specs=P("dp", None), check_vma=False
    )
```

```python
import jax
import jax.numpy as jnp
from jax import lax
from jax.experimental import pallas as pl
from jax.experimental.pallas import tpu as pltpu
from jax.sharding import PartitionSpec as P

EPS = 1e-06
MESH = pl.DeviceIdType.MESH
F32 = jnp.float32
BF16 = jnp.bfloat16

LOCAL = 512
WIDTH = 1024
SIDE = 64
ROWS = LOCAL + SIDE
PANELS = 2
PANEL = LOCAL // PANELS
PIECE = PANEL // 4
HALF = PIECE // 2


def nt(left, right, precision=None):
    return lax.dot_general(
        left, right, (((1,), (1,)), ((), ())), precision=precision, preferred_element_type=F32
    )


def kernel(
    hidden,
    targets_in,
    lengths_in,
    filter_in,
    proj_weight,
    unembed,
    proj_in_t,
    proj_out_t,
    queries,
    out,
    targets,
    lengths,
    conv_filter,
    held,
    mixed,
    weight,
    words,
    words_sib,
    words_far,
    side_in_w,
    side_out_w,
    folded,
    folded_low,
    up_part,
    up_sib,
    up_chip,
    up_far,
    logits_full,
    logits_low,
    from_sib,
    to_near,
    from_near,
    side_t,
    query_all,
    grad_out,
    grad_all,
    grad_rows,
    score_out,
    score_all,
    local_sem,
    uz_send,
    uz_recv,
    us_send,
    us_recv,
    uf_send,
    uf_recv,
    w_send,
    w_recv,
    up_send,
    up_recv,
    a_send,
    a_recv,
    b_send,
    b_recv,
    qz_send,
    qz_recv,
    qx_send,
    qx_recv,
    g_send,
    g_recv,
    s_send,
    s_recv,
):
    dp = lax.axis_index("dp")
    tensor = lax.axis_index("tensor")
    x, y, zh = dp // 16, (dp // 4) % 4, dp % 4
    zl, core = tensor // 2, tensor % 2
    me = y * 4 + tensor
    colours = [(x + 2 * y) % 4, (2 * x + y) % 4]
    pieces = [pl.ds(pl.multiple_of(p * PANEL + colours[p] * PIECE, PIECE), PIECE) for p in range(PANELS)]
    packed = [pl.ds(p * PIECE, PIECE) for p in range(PANELS)]
    far_dp = dp - zh + (zh + 2 * zl + 3) % 4
    sib = (dp, zl * 2 + 1 - core)
    near = (dp, (1 - zl) * 2 + core)
    far = (far_dp, (1 - zl) * 2 + core)

    def at_x(step):
        return (dp - x * 16 + ((x + step) % 4) * 16, tensor)

    def at_y(step):
        return (dp - y * 4 + ((y + step) % 4) * 4, tensor)

    def at_z(step):
        return (dp - zh + (zh + step) % 4, tensor)

    def member(place):
        return (dp - y * 4 + (place // 4) * 4, place % 4)

    def remote(src, dst, send, recv, device):
        return pltpu.make_async_remote_copy(
            src_ref=src, dst_ref=dst, send_sem=send, recv_sem=recv, device_id=device, device_id_type=MESH
        )

    barrier = pltpu.get_barrier_semaphore()
    partners = [far, sib, near, (dp, (1 - zl) * 2 + 1 - core)]
    partners += [at_x(i) for i in (1, 2, 3)] + [at_z(i) for i in (1, 2, 3)]
    partners += [member((me + 4 * turn) % 16 - tensor + (tensor + step) % 4) for turn in (1, 2, 3) for step in range(4)]
    for device in partners:
        pl.semaphore_signal(barrier, inc=1, device_id=device, device_id_type=MESH)

    slices = (tensor, zl * 2 + 1 - core, (1 - zl) * 2 + core, (1 - zl) * 2 + 1 - core)
    own_queries = query_all.at[pl.ds(pl.multiple_of(x * 64 + zh * 16, 16), 16)]

    def x_queries(step, size, first=0):
        return query_all.at[pl.ds(pl.multiple_of((x + step) % 4 * 64 + first, size), size)]

    local = [
        (hidden, held),
        (filter_in, conv_filter),
        (unembed, words),
        (proj_out_t, side_out_w),
    ]
    local += [
        (proj_weight.at[:, pl.ds(pl.multiple_of(slices[i] * WIDTH, WIDTH), WIDTH)], weight.at[i]) for i in range(4)
    ]
    local += [(proj_in_t, side_in_w), (queries, own_queries), (targets_in, targets), (lengths_in, lengths)]
    loads = [pltpu.make_async_copy(src, dst, local_sem.at[i]) for i, (src, dst) in enumerate(local)]
    for i in (2, 4, 5):
        loads[i].start()

    pl.semaphore_wait(barrier, len(partners))

    sends, word_copies, sib_copies = [], [], []
    for p in range(PANELS):
        copies = []
        for side, device in enumerate((near, far)):
            rows = pl.ds(pl.multiple_of(p * PANEL + colours[p] * PIECE + side * HALF, HALF), HALF)
            copy = remote(
                unembed.at[rows],
                words_far.at[0, pl.ds(p * PIECE + side * HALF, HALF)],
                uz_send.at[p, side],
                uz_recv.at[p, side],
                device,
            )
            copy.start()
            copies.append(copy)
        word_copies.append(copies)
        sends.extend(copies)
    for p in range(PANELS):
        copy = remote(unembed.at[pieces[p]], words_sib.at[packed[p]], us_send.at[p], us_recv.at[p], sib)
        copy.start()
        sib_copies.append(copy)
    sends.extend(sib_copies)

    for i in (6, 7, 0, 1, 3, 8, 9, 10, 11):
        loads[i].start()


    loads[2].wait()
    loads[4].wait()
    folded[...] = nt(jnp.concatenate([words[rows] for rows in pieces], axis=0), weight[0])

    a_copies, b_copies = {}, {}
    bands = [pl.ds(i * 128, 128) for i in range(4)] + [pl.ds(LOCAL, SIDE)]

    def send_a(index, part):
        rows = bands[index]
        for quarter in range(4):
            columns = part[:, quarter * 128 : (quarter + 1) * 128]
            logits_full[quarter % 2, quarter // 2, rows] = columns
            logits_low[quarter % 2, quarter // 2, rows] = columns.astype(BF16)
        copy = remote(
            logits_low.at[1 - core, :, rows], from_sib.at[:, rows], a_send.at[index], a_recv.at[index], sib
        )
        copy.start()
        a_copies[index] = copy

    def send_b(index):
        rows = bands[index]
        a_copies[index].wait_recv()
        chip = logits_full[core, 1 - zl, rows] + from_sib[1 - zl, rows].astype(F32)
        to_near[rows] = chip.astype(BF16)
        copy = remote(to_near.at[rows], from_near.at[rows], b_send.at[index], b_recv.at[index], near)
        copy.start()
        b_copies[index] = copy

    for copy in sib_copies:
        copy.wait_recv()
    loads[5].wait()
    folded[...] += nt(words_sib[...], weight[1])

    w_copies, forwards = [], []

    def arrive(p):
        for copy in word_copies[p]:
            copy.wait_recv()
        copy = remote(words_far.at[0, packed[p]], words_far.at[1, packed[p]], uf_send.at[p], uf_recv.at[p], sib)
        copy.start()
        forwards.append(copy)
        folded[packed[p]] += nt(words_far[0, packed[p]], weight[2])

    def fold(p):
        forwards[p].wait_recv()
        part = folded[packed[p]] + nt(words_far[1, packed[p]], weight[3])
        folded_low[pieces[p]] = part.astype(BF16)
        along, across = (at_x, at_y) if p == 0 else (at_y, at_x)
        copies = []
        for i, device in enumerate((along(1), along(3))):
            copies.append(
                remote(folded_low.at[pieces[p]], folded_low.at[pieces[p]], w_send.at[p, i], w_recv.at[p, i], device)
            )
        for i, device in enumerate((across(1), across(3))):
            rows = pl.ds(pl.multiple_of(p * PANEL + colours[p] * PIECE + i * HALF, HALF), HALF)
            copies.append(
                remote(folded_low.at[rows], folded_low.at[rows], w_send.at[p, 2 + i], w_recv.at[p, 2 + i], device)
            )
        for copy in copies:
            copy.start()
        w_copies.append(copies)
        sends.extend(copies)

    def logits_of(p, half):
        if half == 0:
            for copy in w_copies[p]:
                copy.wait_recv()
        index = 2 * p + half
        send_a(index, nt(folded_low[bands[index]], mixed[...]))

    loads[6].wait()
    arrive(0)
    arrive(1)

    loads[7].wait()
    fold(0)
    fold(1)
    sends.extend(forwards)

    loads[9].wait()
    qz_copies = []
    for step in (1, 2, 3):
        copy = remote(queries, own_queries, qz_send.at[step], qz_recv.at[step], at_z(step))
        copy.start()
        qz_copies.append(copy)

    loads[0].wait()
    loads[1].wait()
    chunk = 256
    first_row = lax.broadcasted_iota(jnp.int32, (256, chunk), 0)

    def convolve(i, carry):
        row = i // (WIDTH // chunk)
        columns = pl.ds(pl.multiple_of((i % (WIDTH // chunk)) * chunk, chunk), chunk)
        values = held[row, :, columns].astype(F32)
        taps = conv_filter[:, columns].astype(F32)
        first = jnp.where(first_row < 1, 0.0, pltpu.roll(values, 1, 0))
        second = jnp.where(first_row < 2, 0.0, pltpu.roll(values, 2, 0))
        result = taps[0:1] * values + taps[1:2] * first + taps[2:3] * second
        mixed[pl.ds(pl.multiple_of(row * 256, 256), 256), columns] = result.astype(BF16)
        return carry

    lax.fori_loop(0, 2 * (WIDTH // chunk), convolve, 0)

    loads[3].wait()
    up_part[...] = nt(side_out_w[...], words[...])
    up_to_sib = remote(up_part, up_sib, up_send.at[0], up_recv.at[0], sib)
    up_to_sib.start()
    sends.append(up_to_sib)

    loads[8].wait()
    send_a(4, nt(side_in_w[...], mixed[...]))

    up_to_sib.wait_recv()
    up_chip[...] = up_part[...] + up_sib[...]
    up_copies = []
    for side, device in enumerate((near, far)):
        rows = pl.ds(side * (SIDE // 2), SIDE // 2)
        copy = remote(up_chip.at[rows], up_far.at[rows], up_send.at[1 + side], up_recv.at[1 + side], device)
        copy.start()
        up_copies.append(copy)
    sends.extend(up_copies)
    send_b(4)

    logits_of(0, 0)
    logits_of(0, 1)
    for copy in qz_copies:
        copy.wait_recv()
    qx_copies = []
    for step in (1, 3):
        copy = remote(x_queries(0, 64), x_queries(0, 64), qx_send.at[step], qx_recv.at[step], at_x(step))
        copy.start()
        qx_copies.append(copy)
    logits_of(1, 0)
    send_b(0)
    logits_of(1, 1)
    send_b(1)
    send_b(2)
    send_b(3)
    for copy in qx_copies:
        copy.wait_recv()
    for i, (step, source, first) in enumerate(((1, 3, 0), (3, 1, 32))):
        rows = x_queries(source, 32, first)
        copy = remote(rows, rows, qx_send.at[2 * i], qx_recv.at[2 * i], at_x(step))
        copy.start()
        qx_copies.append(copy)
    sends.extend(qz_copies + qx_copies)
    sends.extend(list(a_copies.values()) + list(b_copies.values()))

    for copy in up_copies:
        copy.wait_recv()
    up = (up_chip[...] + up_far[...]).astype(BF16)
    for copy in b_copies.values():
        copy.wait_recv()
    total = logits_full[core, zl] + from_sib[zl].astype(F32) + from_near[...].astype(F32)
    expo = jnp.exp(total[:LOCAL])
    prob = expo / jnp.sum(expo, axis=0, keepdims=True)
    loads[10].wait()
    loads[11].wait()
    position = lax.broadcasted_iota(jnp.int32, (1, 128), 1) + core * 128
    live = (position < lengths[zl]).astype(F32)
    ids = [jnp.where(zl == 0, targets[0:1, i : i + 128], targets[1:2, i : i + 128]) for i in (0, 128)]
    target = jnp.where(core == 0, ids[0], ids[1])
    onehot = (lax.broadcasted_iota(jnp.int32, (LOCAL, 128), 0) == target).astype(F32)
    grad_logits = ((prob - onehot) * live).astype(BF16)
    side_out = jnp.dot(up, grad_logits, preferred_element_type=F32)
    side_t[...] = total[LOCAL:]
    even = nt(side_t[pl.ds(0, SIDE // 2, stride=2), :], side_out, lax.Precision.HIGHEST)
    odd = nt(side_t[pl.ds(1, SIDE // 2, stride=2), :], side_out, lax.Precision.HIGHEST)
    row_grad = jnp.concatenate([even, odd], axis=1)
    for share in range(4):
        grad_out[share] = row_grad[share * 8 : (share + 1) * 8]

    order = [(me + 4 * turn) % 16 - tensor + (tensor + step) % 4 for turn in (2, 1, 3) for step in range(4)]
    order += [me - tensor + (tensor + step) % 4 for step in (1, 2, 3)]
    tail = grad_all.at[pl.ds(0, 15)]

    grad_all[me] = grad_out[tensor]
    grad_copies = []
    for place in order:
        copy = remote(grad_out.at[place % 4], grad_all.at[me], g_send, g_recv, member(place))
        copy.start()
        grad_copies.append(copy)
    for copy in qx_copies[2:]:
        copy.wait_recv()
    pltpu.make_async_copy(tail, tail, g_recv).wait()

    norms = []
    for row in range(8):
        whole = grad_all[2 * row] + grad_all[2 * row + 1]
        grad_rows[pl.ds(row * 8, 8)] = whole
        norms.append(jnp.sum(whole * whole, axis=(0, 1), keepdims=True))
    flat = jnp.concatenate([grad_rows[pl.ds(i, 8, stride=8), :] for i in range(8)], axis=1).astype(BF16)
    scores = nt(flat, query_all[...])
    for row in range(8):
        for half in range(2):
            score_out[row // 2, pl.ds((row % 2) * 2 + half, 1)] = scores[
                row : row + 1, half * 128 : (half + 1) * 128
            ]
            score_out[row // 2, pl.ds(4 + (row % 2) * 2 + half, 1)] = jnp.broadcast_to(norms[row], (1, 128))

    score_all[me] = score_out[y]
    score_copies = []
    for place in order:
        copy = remote(score_out.at[place // 4], score_all.at[me], s_send, s_recv, member(place))
        copy.start()
        score_copies.append(copy)
    pltpu.make_async_copy(tail, tail, s_recv).wait()

    sums = [score_all[4 * i] + score_all[4 * i + 1] + score_all[4 * i + 2] + score_all[4 * i + 3] for i in range(4)]
    scale = jnp.sqrt(sums[0][4:8] + EPS)
    low_lanes = lax.broadcasted_iota(jnp.int32, (8, 128), 1) < 64
    turned = [pltpu.roll(part, 64, 1) for part in sums]
    for odd_x in range(2):
        for pair in range(2):
            left = (turned if odd_x else sums)[2 * pair]
            right = (sums if odd_x else turned)[2 * pair + 1]
            line = jnp.where(low_lanes, left, right)[0:4] / scale
            for row in range(2):
                for half in range(2):
                    column = 128 * (4 * half + 2 * odd_x + pair)
                    out[pl.ds(row, 1), pl.ds(column, 128)] = line[2 * row + half : 2 * row + half + 1]

    for sem in (g_send, s_send):
        pltpu.make_async_copy(tail, tail, sem).wait()
    for copy in sends:
        copy.wait_send()


def per_device(hidden, targets, lengths, conv_filter, proj_weight, unembed, proj_in, proj_out, query_grads):
    hbm = pl.BlockSpec(memory_space=pltpu.HBM)
    vmem = pl.BlockSpec(memory_space=pltpu.VMEM)
    dma = pltpu.SemaphoreType.DMA
    scratch = [
        pltpu.VMEM((2, 256), jnp.int32),
        pltpu.SMEM((2,), jnp.int32),
        pltpu.VMEM((3, WIDTH), BF16),
        pltpu.VMEM((2, 256, WIDTH), BF16),
        pltpu.VMEM((LOCAL, WIDTH), BF16),
        pltpu.VMEM((4, WIDTH, WIDTH), BF16),
        pltpu.VMEM((LOCAL, WIDTH), BF16),
        pltpu.VMEM((PANELS * PIECE, WIDTH), BF16),
        pltpu.VMEM((2, PANELS * PIECE, WIDTH), BF16),
        pltpu.VMEM((SIDE, WIDTH), BF16),
        pltpu.VMEM((SIDE, WIDTH), BF16),
        pltpu.VMEM((PANELS * PIECE, WIDTH), F32),
        pltpu.VMEM((LOCAL, WIDTH), BF16),
        pltpu.VMEM((SIDE, LOCAL), F32),
        pltpu.VMEM((SIDE, LOCAL), F32),
        pltpu.VMEM((SIDE, LOCAL), F32),
        pltpu.VMEM((SIDE, LOCAL), F32),
        pltpu.VMEM((2, 2, ROWS, 128), F32),
        pltpu.VMEM((2, 2, ROWS, 128), BF16),
        pltpu.VMEM((2, ROWS, 128), BF16),
        pltpu.VMEM((ROWS, 128), BF16),
        pltpu.VMEM((ROWS, 128), BF16),
        pltpu.VMEM((SIDE, 128), F32),
        pltpu.VMEM((256, WIDTH), BF16),
        pltpu.VMEM((4, 8, 128), F32),
        pltpu.VMEM((16, 8, 128), F32),
        pltpu.VMEM((64, 128), F32),
        pltpu.VMEM((4, 8, 128), F32),
        pltpu.VMEM((16, 8, 128), F32),
        dma((12,)),
        dma((PANELS, 2)),
        dma((PANELS, 2)),
        dma((PANELS,)),
        dma((PANELS,)),
        dma((PANELS,)),
        dma((PANELS,)),
        dma((PANELS, 4)),
        dma((PANELS, 4)),
        dma((3,)),
        dma((3,)),
        dma((5,)),
        dma((5,)),
        dma((5,)),
        dma((5,)),
        dma((4,)),
        dma((4,)),
        dma((4,)),
        dma((4,)),
        dma,
        dma,
        dma,
        dma,
    ]
    return pl.pallas_call(
        kernel,
        out_shape=jax.ShapeDtypeStruct((2, 1024), F32),
        in_specs=[hbm] * 9,
        out_specs=vmem,
        scratch_shapes=scratch,
        compiler_params=pltpu.CompilerParams(
            collective_id=0, has_side_effects=True, vmem_limit_bytes=64 * 1024 * 1024
        ),
        name="attribution",
    )(hidden, targets, lengths, conv_filter, proj_weight, unembed, proj_in.T, proj_out.T, query_grads)


def solution(mesh):
    in_specs = (
        P("dp", None, "tensor"),
        P("dp", None),
        P("dp"),
        P(None, "tensor"),
        P("tensor", None),
        P(None, "tensor"),
        P("tensor", None),
        P("tensor", None),
        P("dp", "tensor"),
    )
    return jax.shard_map(
        per_device, mesh=mesh, in_specs=in_specs, out_specs=P("dp", None), check_vma=False
    )
```

```python
import jax
import jax.numpy as jnp
from jax import lax
from jax.experimental import pallas as pl
from jax.experimental.pallas import tpu as pltpu
from jax.sharding import PartitionSpec as P

EPS = 1e-06
MESH = pl.DeviceIdType.MESH
F32 = jnp.float32
BF16 = jnp.bfloat16

LOCAL = 512
WIDTH = 1024
SIDE = 64
ROWS = LOCAL + SIDE
PANELS = 2
PANEL = LOCAL // PANELS
PIECE = PANEL // 4
HALF = PIECE // 2


def nt(left, right, precision=None):
    return lax.dot_general(
        left, right, (((1,), (1,)), ((), ())), precision=precision, preferred_element_type=F32
    )


def kernel(
    hidden,
    targets_in,
    lengths_in,
    filter_in,
    proj_weight,
    unembed,
    proj_in_t,
    proj_out_t,
    queries,
    out,
    targets,
    lengths,
    conv_filter,
    held,
    mixed,
    weight,
    words,
    words_sib,
    words_far,
    side_in_w,
    side_out_w,
    folded,
    folded_low,
    up_part,
    up_sib,
    up_chip,
    up_far,
    logits_full,
    logits_low,
    from_sib,
    to_near,
    from_near,
    side_t,
    query_all,
    grad_out,
    grad_all,
    grad_rows,
    score_out,
    score_all,
    local_sem,
    uz_send,
    uz_recv,
    us_send,
    us_recv,
    uf_send,
    uf_recv,
    w_send,
    w_recv,
    up_send,
    up_recv,
    a_send,
    a_recv,
    b_send,
    b_recv,
    qz_send,
    qz_recv,
    qx_send,
    qx_recv,
    g_send,
    g_recv,
    s_send,
    s_recv,
):
    dp = lax.axis_index("dp")
    tensor = lax.axis_index("tensor")
    x, y, zh = dp // 16, (dp // 4) % 4, dp % 4
    zl, core = tensor // 2, tensor % 2
    me = y * 4 + tensor
    colours = [(x + 2 * y) % 4, (2 * x + y) % 4]
    pieces = [pl.ds(pl.multiple_of(p * PANEL + colours[p] * PIECE, PIECE), PIECE) for p in range(PANELS)]
    packed = [pl.ds(p * PIECE, PIECE) for p in range(PANELS)]
    far_dp = dp - zh + (zh + 2 * zl + 3) % 4
    sib = (dp, zl * 2 + 1 - core)
    near = (dp, (1 - zl) * 2 + core)
    far = (far_dp, (1 - zl) * 2 + core)

    def at_x(step):
        return (dp - x * 16 + ((x + step) % 4) * 16, tensor)

    def at_y(step):
        return (dp - y * 4 + ((y + step) % 4) * 4, tensor)

    def at_z(step):
        return (dp - zh + (zh + step) % 4, tensor)

    def member(place):
        return (dp - y * 4 + (place // 4) * 4, place % 4)

    def remote(src, dst, send, recv, device):
        return pltpu.make_async_remote_copy(
            src_ref=src, dst_ref=dst, send_sem=send, recv_sem=recv, device_id=device, device_id_type=MESH
        )

    barrier = pltpu.get_barrier_semaphore()
    partners = [at_z(2), at_z(1), at_z(3)]
    partners += [member((me + 4 * turn) % 16 - tensor + (tensor + step) % 4) for turn in (2, 1, 3) for step in range(4)]
    partners += [at_x(1), at_x(3), far, (dp, (1 - zl) * 2 + 1 - core), near, sib]
    for device in partners:
        pl.semaphore_signal(barrier, inc=1, device_id=device, device_id_type=MESH)

    slices = (tensor, zl * 2 + 1 - core, (1 - zl) * 2 + core, (1 - zl) * 2 + 1 - core)
    own_queries = query_all.at[pl.ds(pl.multiple_of(x * 64 + zh * 16, 16), 16)]

    def x_queries(step, size, first=0):
        return query_all.at[pl.ds(pl.multiple_of((x + step) % 4 * 64 + first, size), size)]

    local = [
        (hidden, held),
        (filter_in, conv_filter),
        (unembed, words),
        (proj_out_t, side_out_w),
    ]
    local += [
        (proj_weight.at[:, pl.ds(pl.multiple_of(slices[i] * WIDTH, WIDTH), WIDTH)], weight.at[i]) for i in range(4)
    ]
    local += [(proj_in_t, side_in_w), (queries, own_queries), (targets_in, targets), (lengths_in, lengths)]
    loads = [pltpu.make_async_copy(src, dst, local_sem.at[i]) for i, (src, dst) in enumerate(local)]
    for i in (2, 4, 5):
        loads[i].start()

    pl.semaphore_wait(barrier, len(partners))

    sends, word_copies, sib_copies = [], [], []
    for p in range(PANELS):
        copies = []
        for side, device in enumerate((near, far)):
            rows = pl.ds(pl.multiple_of(p * PANEL + colours[p] * PIECE + side * HALF, HALF), HALF)
            copy = remote(
                unembed.at[rows],
                words_far.at[0, pl.ds(p * PIECE + side * HALF, HALF)],
                uz_send.at[p, side],
                uz_recv.at[p, side],
                device,
            )
            copy.start()
            copies.append(copy)
        word_copies.append(copies)
        sends.extend(copies)
    for p in range(PANELS):
        copy = remote(unembed.at[pieces[p]], words_sib.at[packed[p]], us_send.at[p], us_recv.at[p], sib)
        copy.start()
        sib_copies.append(copy)
    sends.extend(sib_copies)

    for i in (6, 7, 0, 1, 3, 8, 9, 10, 11):
        loads[i].start()


    loads[2].wait()
    loads[4].wait()
    folded[...] = nt(jnp.concatenate([words[rows] for rows in pieces], axis=0), weight[0])

    a_copies, b_copies = {}, {}
    bands = [pl.ds(p * PANEL, PANEL) for p in range(PANELS)] + [pl.ds(LOCAL, SIDE)]

    def send_a(index, part):
        rows = bands[index]
        for quarter in range(4):
            columns = part[:, quarter * 128 : (quarter + 1) * 128]
            logits_full[quarter % 2, quarter // 2, rows] = columns
            logits_low[quarter % 2, quarter // 2, rows] = columns.astype(BF16)
        copy = remote(
            logits_low.at[1 - core, :, rows], from_sib.at[:, rows], a_send.at[index], a_recv.at[index], sib
        )
        copy.start()
        a_copies[index] = copy

    def send_b(index):
        rows = bands[index]
        a_copies[index].wait_recv()
        chip = logits_full[core, 1 - zl, rows] + from_sib[1 - zl, rows].astype(F32)
        to_near[rows] = chip.astype(BF16)
        copy = remote(to_near.at[rows], from_near.at[rows], b_send.at[index], b_recv.at[index], near)
        copy.start()
        b_copies[index] = copy

    for copy in sib_copies:
        copy.wait_recv()
    loads[5].wait()
    folded[...] += nt(words_sib[...], weight[1])

    w_copies, forwards = [], []

    def arrive(p):
        for copy in word_copies[p]:
            copy.wait_recv()
        copy = remote(words_far.at[0, packed[p]], words_far.at[1, packed[p]], uf_send.at[p], uf_recv.at[p], sib)
        copy.start()
        forwards.append(copy)
        folded[packed[p]] += nt(words_far[0, packed[p]], weight[2])

    def fold(p):
        forwards[p].wait_recv()
        part = folded[packed[p]] + nt(words_far[1, packed[p]], weight[3])
        folded_low[pieces[p]] = part.astype(BF16)
        along, across = (at_x, at_y) if p == 0 else (at_y, at_x)
        copies = []
        for i, device in enumerate((along(1), along(3))):
            copies.append(
                remote(folded_low.at[pieces[p]], folded_low.at[pieces[p]], w_send.at[p, i], w_recv.at[p, i], device)
            )
        for i, device in enumerate((across(1), across(3))):
            rows = pl.ds(pl.multiple_of(p * PANEL + colours[p] * PIECE + i * HALF, HALF), HALF)
            copies.append(
                remote(folded_low.at[rows], folded_low.at[rows], w_send.at[p, 2 + i], w_recv.at[p, 2 + i], device)
            )
        for copy in copies:
            copy.start()
        w_copies.append(copies)
        sends.extend(copies)

    def logits_of(p):
        for copy in w_copies[p]:
            copy.wait_recv()
        send_a(p, nt(folded_low[bands[p]], mixed[...]))

    loads[6].wait()
    arrive(0)

    loads[9].wait()
    qz_copies = []
    for step in (1, 2, 3):
        copy = remote(queries, own_queries, qz_send.at[step], qz_recv.at[step], at_z(step))
        copy.start()
        qz_copies.append(copy)

    arrive(1)

    loads[7].wait()
    fold(0)
    fold(1)
    sends.extend(forwards)

    loads[3].wait()
    up_part[...] = nt(side_out_w[...], words[...])
    up_to_sib = remote(up_part, up_sib, up_send.at[0], up_recv.at[0], sib)
    up_to_sib.start()
    sends.append(up_to_sib)

    loads[0].wait()
    loads[1].wait()
    chunk = 256
    first_row = lax.broadcasted_iota(jnp.int32, (256, chunk), 0)

    def convolve(i, carry):
        row = i // (WIDTH // chunk)
        columns = pl.ds(pl.multiple_of((i % (WIDTH // chunk)) * chunk, chunk), chunk)
        values = held[row, :, columns].astype(F32)
        taps = conv_filter[:, columns].astype(F32)
        first = jnp.where(first_row < 1, 0.0, pltpu.roll(values, 1, 0))
        second = jnp.where(first_row < 2, 0.0, pltpu.roll(values, 2, 0))
        result = taps[0:1] * values + taps[1:2] * first + taps[2:3] * second
        mixed[pl.ds(pl.multiple_of(row * 256, 256), 256), columns] = result.astype(BF16)
        return carry

    lax.fori_loop(0, 2 * (WIDTH // chunk), convolve, 0)

    loads[8].wait()
    send_a(2, nt(side_in_w[...], mixed[...]))

    up_to_sib.wait_recv()
    up_chip[...] = up_part[...] + up_sib[...]
    up_copies = []
    for side, device in enumerate((near, far)):
        rows = pl.ds(side * (SIDE // 2), SIDE // 2)
        copy = remote(up_chip.at[rows], up_far.at[rows], up_send.at[1 + side], up_recv.at[1 + side], device)
        copy.start()
        up_copies.append(copy)
    sends.extend(up_copies)

    logits_of(0)
    send_b(2)
    for copy in qz_copies:
        copy.wait_recv()
    qx_copies = []
    for step in (1, 3):
        copy = remote(x_queries(0, 64), x_queries(0, 64), qx_send.at[step], qx_recv.at[step], at_x(step))
        copy.start()
        qx_copies.append(copy)
    logits_of(1)
    send_b(0)
    send_b(1)
    for copy in qx_copies:
        copy.wait_recv()
    for i, (step, source, first) in enumerate(((1, 3, 0), (3, 1, 32))):
        rows = x_queries(source, 32, first)
        copy = remote(rows, rows, qx_send.at[2 * i], qx_recv.at[2 * i], at_x(step))
        copy.start()
        qx_copies.append(copy)
    sends.extend(qz_copies + qx_copies)
    sends.extend(list(a_copies.values()) + list(b_copies.values()))

    for copy in up_copies:
        copy.wait_recv()
    up = (up_chip[...] + up_far[...]).astype(BF16)
    for copy in b_copies.values():
        copy.wait_recv()
    total = logits_full[core, zl] + from_sib[zl].astype(F32) + from_near[...].astype(F32)
    expo = jnp.exp(total[:LOCAL])
    prob = expo / jnp.sum(expo, axis=0, keepdims=True)
    loads[10].wait()
    loads[11].wait()
    position = lax.broadcasted_iota(jnp.int32, (1, 128), 1) + core * 128
    live = (position < lengths[zl]).astype(F32)
    ids = [jnp.where(zl == 0, targets[0:1, i : i + 128], targets[1:2, i : i + 128]) for i in (0, 128)]
    target = jnp.where(core == 0, ids[0], ids[1])
    onehot = (lax.broadcasted_iota(jnp.int32, (LOCAL, 128), 0) == target).astype(F32)
    grad_logits = ((prob - onehot) * live).astype(BF16)
    side_out = jnp.dot(up, grad_logits, preferred_element_type=F32)
    side_t[...] = total[LOCAL:]
    even = nt(side_t[pl.ds(0, SIDE // 2, stride=2), :], side_out, lax.Precision.HIGHEST)
    odd = nt(side_t[pl.ds(1, SIDE // 2, stride=2), :], side_out, lax.Precision.HIGHEST)
    row_grad = jnp.concatenate([even, odd], axis=1)
    for share in range(4):
        grad_out[share] = row_grad[share * 8 : (share + 1) * 8]

    order = [(me + 4 * turn) % 16 - tensor + (tensor + step) % 4 for turn in (2, 1, 3) for step in range(4)]
    order += [me - tensor + (tensor + step) % 4 for step in (1, 2, 3)]
    tail = grad_all.at[pl.ds(0, 15)]

    grad_all[me] = grad_out[tensor]
    grad_copies = []
    for place in order:
        copy = remote(grad_out.at[place % 4], grad_all.at[me], g_send, g_recv, member(place))
        copy.start()
        grad_copies.append(copy)
    for copy in qx_copies[2:]:
        copy.wait_recv()
    pltpu.make_async_copy(tail, tail, g_recv).wait()

    norms = []
    for row in range(8):
        whole = grad_all[2 * row] + grad_all[2 * row + 1]
        grad_rows[pl.ds(row * 8, 8)] = whole
        norms.append(jnp.sum(whole * whole, axis=(0, 1), keepdims=True))
    flat = jnp.concatenate([grad_rows[pl.ds(i, 8, stride=8), :] for i in range(8)], axis=1).astype(BF16)
    scores = nt(flat, query_all[...])
    for row in range(8):
        for half in range(2):
            score_out[row // 2, pl.ds((row % 2) * 2 + half, 1)] = scores[
                row : row + 1, half * 128 : (half + 1) * 128
            ]
            score_out[row // 2, pl.ds(4 + (row % 2) * 2 + half, 1)] = jnp.broadcast_to(norms[row], (1, 128))

    score_all[me] = score_out[y]
    score_copies = []
    for place in order:
        copy = remote(score_out.at[place // 4], score_all.at[me], s_send, s_recv, member(place))
        copy.start()
        score_copies.append(copy)
    pltpu.make_async_copy(tail, tail, s_recv).wait()

    sums = [score_all[4 * i] + score_all[4 * i + 1] + score_all[4 * i + 2] + score_all[4 * i + 3] for i in range(4)]
    scale = jnp.sqrt(sums[0][4:8] + EPS)
    low_lanes = lax.broadcasted_iota(jnp.int32, (8, 128), 1) < 64
    turned = [pltpu.roll(part, 64, 1) for part in sums]
    for odd_x in range(2):
        for pair in range(2):
            left = (turned if odd_x else sums)[2 * pair]
            right = (sums if odd_x else turned)[2 * pair + 1]
            line = jnp.where(low_lanes, left, right)[0:4] / scale
            for row in range(2):
                for half in range(2):
                    column = 128 * (4 * half + 2 * odd_x + pair)
                    out[pl.ds(row, 1), pl.ds(column, 128)] = line[2 * row + half : 2 * row + half + 1]

    for sem in (g_send, s_send):
        pltpu.make_async_copy(tail, tail, sem).wait()
    for copy in sends:
        copy.wait_send()


def per_device(hidden, targets, lengths, conv_filter, proj_weight, unembed, proj_in, proj_out, query_grads):
    hbm = pl.BlockSpec(memory_space=pltpu.HBM)
    vmem = pl.BlockSpec(memory_space=pltpu.VMEM)
    dma = pltpu.SemaphoreType.DMA
    scratch = [
        pltpu.VMEM((2, 256), jnp.int32),
        pltpu.SMEM((2,), jnp.int32),
        pltpu.VMEM((3, WIDTH), BF16),
        pltpu.VMEM((2, 256, WIDTH), BF16),
        pltpu.VMEM((LOCAL, WIDTH), BF16),
        pltpu.VMEM((4, WIDTH, WIDTH), BF16),
        pltpu.VMEM((LOCAL, WIDTH), BF16),
        pltpu.VMEM((PANELS * PIECE, WIDTH), BF16),
        pltpu.VMEM((2, PANELS * PIECE, WIDTH), BF16),
        pltpu.VMEM((SIDE, WIDTH), BF16),
        pltpu.VMEM((SIDE, WIDTH), BF16),
        pltpu.VMEM((PANELS * PIECE, WIDTH), F32),
        pltpu.VMEM((LOCAL, WIDTH), BF16),
        pltpu.VMEM((SIDE, LOCAL), F32),
        pltpu.VMEM((SIDE, LOCAL), F32),
        pltpu.VMEM((SIDE, LOCAL), F32),
        pltpu.VMEM((SIDE, LOCAL), F32),
        pltpu.VMEM((2, 2, ROWS, 128), F32),
        pltpu.VMEM((2, 2, ROWS, 128), BF16),
        pltpu.VMEM((2, ROWS, 128), BF16),
        pltpu.VMEM((ROWS, 128), BF16),
        pltpu.VMEM((ROWS, 128), BF16),
        pltpu.VMEM((SIDE, 128), F32),
        pltpu.VMEM((256, WIDTH), BF16),
        pltpu.VMEM((4, 8, 128), F32),
        pltpu.VMEM((16, 8, 128), F32),
        pltpu.VMEM((64, 128), F32),
        pltpu.VMEM((4, 8, 128), F32),
        pltpu.VMEM((16, 8, 128), F32),
        dma((12,)),
        dma((PANELS, 2)),
        dma((PANELS, 2)),
        dma((PANELS,)),
        dma((PANELS,)),
        dma((PANELS,)),
        dma((PANELS,)),
        dma((PANELS, 4)),
        dma((PANELS, 4)),
        dma((3,)),
        dma((3,)),
        dma((3,)),
        dma((3,)),
        dma((3,)),
        dma((3,)),
        dma((4,)),
        dma((4,)),
        dma((4,)),
        dma((4,)),
        dma,
        dma,
        dma,
        dma,
    ]
    return pl.pallas_call(
        kernel,
        out_shape=jax.ShapeDtypeStruct((2, 1024), F32),
        in_specs=[hbm] * 9,
        out_specs=vmem,
        scratch_shapes=scratch,
        compiler_params=pltpu.CompilerParams(
            collective_id=0, has_side_effects=True, vmem_limit_bytes=64 * 1024 * 1024
        ),
        name="attribution",
    )(hidden, targets, lengths, conv_filter, proj_weight, unembed, proj_in.T, proj_out.T, query_grads)


def solution(mesh):
    in_specs = (
        P("dp", None, "tensor"),
        P("dp", None),
        P("dp"),
        P(None, "tensor"),
        P("tensor", None),
        P(None, "tensor"),
        P("tensor", None),
        P("tensor", None),
        P("dp", "tensor"),
    )
    return jax.shard_map(
        per_device, mesh=mesh, in_specs=in_specs, out_specs=P("dp", None), check_vma=False
    )
```
